32 devices in a mesh: groups: 2 (over x), var: 16 (over z, y, core).
Axes of the slice: x: 2, y: 2, z: 4, core: 2. Of those that a mesh axis runs over, the one named last changes fastest.
Arguments:
- samples: bfloat16 [2048, 57344], P('groups', 'var'), parts along dimension 0, may hold values from -6 to 6
- omega: float32 [4480, 128, 128], P(('groups', 'var')), parts along dimension 0, as said below
- block_rows: int32 [4480], P(('groups', 'var')), parts along dimension 0, may hold values from -1 to 447, as said below
- block_cols: int32 [4480], P(('groups', 'var')), parts along dimension 0, may hold values from -1 to 447, as said below
- block_count: int32 [32], P(('groups', 'var')), parts along dimension 0, may hold values from 28 to 140, as said below
Outputs:
- new_omega: float32 [4480, 128, 128], P(('groups', 'var')), parts along dimension 0
- objective: float32 [2], P('groups'), parts along dimension 0
The draws below stay inside these ranges and needn't reach their ends.
There are 2 independent parts, one for each index of `groups`. The reference program is written for one: setup_inputs(seed, part) draws one part's arguments, and reference() takes and returns one part's arrays. A program takes and returns all parts, laid end to end along the dimension named above; each array names one. Nothing has to cross between parts.
Inputs may be any that keep to these rules, and one draw needn't show every extreme that they name: `block_rows`: the support is symmetric, holds every diagonal block, and every support block lies within 2 column blocks of its column block around the circle of 448 blocks, with the rows wrapping from 447 to 0. The live slots of a device come first and name blocks of its own columns, each block once; slots past the count hold -1. `block_cols`: column block of each live slot, one of the device's own 28 consecutive column blocks; -1 past the count. `block_count`: some device holds 140 live slots. The blocks of omega form a symmetric matrix: the block at (i, j) is the transpose of the block at (j, i). Its diagonal entries lie in 1 to 3. Slots past the count hold zeros.
All inputs are finite; a program needn't handle non-finite values.
Results may differ from the reference program's by a relative error of at most 0.0032.
Values may be sent and summed in bfloat16 or wider, within the bound.
A program may use at most 192 MiB of HBM per device.

```python
import jax
import jax.numpy as jnp
from jax import lax

P_SIZE = 57344
BLK = 128
KB = 2
SAMPLES = 1024
CB = 28
BMAX = 140


def support_tables(key):
    nblocks = P_SIZE // BLK
    devices = nblocks // CB
    width_band = 2 * KB + 1
    per_device = CB * width_band
    heavy = jax.random.randint(jax.random.fold_in(key, 101), (), 0, devices)
    coins = jax.random.randint(jax.random.fold_in(key, 102), (KB, nblocks), 0, 100) < 50
    columns = jnp.arange(nblocks, dtype=jnp.int32)
    owners = columns // CB
    distance = jnp.arange(1, KB + 1, dtype=jnp.int32)
    ahead = jnp.mod(columns[None, :] + distance[:, None], nblocks)
    edges = coins | (owners[None, :] == heavy) | (ahead // CB == heavy)
    behind = jnp.mod(columns[None, :] - distance[:, None], nblocks)
    upper = edges.T
    lower = jnp.take_along_axis(edges, behind, axis=1).T
    active = jnp.concatenate([lower[:, ::-1], jnp.ones((nblocks, 1), bool), upper], axis=1)
    offsets = jnp.arange(width_band, dtype=jnp.int32) - KB
    row_table = jnp.mod(columns[:, None] + offsets[None, :], nblocks)
    col_table = jnp.broadcast_to(columns[:, None], (nblocks, width_band))
    active = active.reshape(devices, per_device)
    row_table = row_table.reshape(devices, per_device)
    col_table = col_table.reshape(devices, per_device)
    candidate = jnp.arange(per_device, dtype=jnp.int32)
    scores = jnp.where(active, 0, per_device) + candidate[None, :]
    order = jnp.argsort(scores, axis=1)
    sorted_active = jnp.take_along_axis(active, order, axis=1)
    rows = jnp.where(sorted_active, jnp.take_along_axis(row_table, order, axis=1), -1)
    cols = jnp.where(sorted_active, jnp.take_along_axis(col_table, order, axis=1), -1)
    counts = jnp.sum(active.astype(jnp.int32), axis=1).astype(jnp.int32)
    return (rows.reshape(-1).astype(jnp.int32), cols.reshape(-1).astype(jnp.int32), counts)


def draw_block_rows(key, part):
    rows, cols, counts = support_tables(key)
    return rows


def draw_block_cols(key, part):
    rows, cols, counts = support_tables(key)
    return cols


def draw_block_count(key, part):
    rows, cols, counts = support_tables(key)
    return counts


def make_block(float_key, pair_id, flipped, on_diagonal, spread, diag_top):
    block_key = jax.random.fold_in(float_key, pair_id)
    raw = jax.random.uniform(block_key, (BLK, BLK), jnp.float32, -spread, spread)
    raw = raw + 0.1 * jax.random.normal(jax.random.fold_in(block_key, 5), (BLK, BLK), jnp.float32) * (spread < 0.15)
    symmetric = (raw + raw.T) * 0.5
    diagonal_values = jax.random.uniform(jax.random.fold_in(block_key, 9), (BLK,), jnp.float32, 1.0, diag_top)
    identity = jnp.eye(BLK, dtype=jnp.float32)
    diagonal_block = symmetric * (1.0 - identity) + identity * diagonal_values[None, :]
    drawn = jnp.where(flipped, raw.T, raw)
    return jnp.where(on_diagonal, diagonal_block, drawn)


def draw_omega(key, part):
    rows, cols, counts = support_tables(key)
    key = jax.random.fold_in(key, 7)
    nblocks = P_SIZE // BLK
    per_device = CB * (2 * KB + 1)
    slot_index = jnp.arange(rows.shape[0], dtype=jnp.int32)
    slot_live = slot_index % per_device < counts[slot_index // per_device]
    lower_id = jnp.minimum(rows, cols)
    upper_id = jnp.maximum(rows, cols)
    pair_id = jnp.where(slot_live, lower_id * nblocks + upper_id, 0)
    flipped = rows > cols
    on_diagonal = rows == cols
    spread = 0.0
    diag_top = 2.0
    blocks = jax.vmap(lambda pid, flp, dia: make_block(key, pid, flp, dia, spread, diag_top))(pair_id, flipped, on_diagonal)
    return blocks * slot_live.astype(jnp.float32)[:, None, None]


def steps_of(stream_key, dims, cuts, smallest, top_value):
    factor_of, own = 1.0, jax.random.fold_in(stream_key, 6)
    for dim, parts in cuts:
        steps = jnp.exp(jax.random.uniform(jax.random.fold_in(own, dim), (parts,), jnp.float32, smallest / len(cuts), top_value / len(cuts)))
        factor_of = factor_of * jnp.repeat(steps, dims[dim] // parts).reshape([-1 if axis == dim else 1 for axis in range(len(dims))])
    return factor_of


def centred(own_key, dims, deviation, most, shards=(), kind=jnp.bfloat16):
    gain = steps_of(own_key, dims, shards, -0.22, 0.18) if shards else 1.0
    values = jax.random.normal(own_key, dims, jnp.float32) * deviation * gain
    return jnp.minimum(jnp.maximum(values, -most), most).astype(kind)


def setup_inputs(seed: int = 0, part: int = 0) -> dict:
    arg_keys = jax.random.split(jax.random.key(seed), 6)
    part_splits = jax.random.split(jax.random.fold_in(arg_keys[5], part), 6)
    samples = centred(part_splits[0], (SAMPLES, P_SIZE), 1.0, 6.0, ((1, 16),))
    omega = draw_omega(jax.random.fold_in(jax.random.fold_in(arg_keys[5], part), 71), part)
    block_rows = draw_block_rows(jax.random.fold_in(jax.random.fold_in(arg_keys[5], part), 71), part)
    block_cols = draw_block_cols(jax.random.fold_in(jax.random.fold_in(arg_keys[5], part), 71), part)
    block_count = draw_block_count(jax.random.fold_in(jax.random.fold_in(arg_keys[5], part), 71), part)
    return {"samples": samples, "omega": omega, "block_rows": block_rows, "block_cols": block_cols, "block_count": block_count}


step_size = 0.5
penalty = 0.1


def reference(samples, omega, block_rows, block_cols, block_count):
    width_band = 2 * KB + 1
    nblocks = P_SIZE // BLK
    total_slots = omega.shape[0]
    slot_index = jnp.arange(total_slots, dtype=jnp.int32)
    owner = slot_index // BMAX
    slot_live = (slot_index % BMAX) < block_count[owner]
    offset_index = jnp.mod(block_rows - block_cols + KB, nblocks)
    outside = nblocks * width_band
    position = jnp.where(slot_live, block_cols * width_band + offset_index, outside).astype(jnp.int32)
    banded = jnp.zeros((outside, BLK, BLK), jnp.float32).at[position].set(omega, mode="drop")
    present = jnp.zeros((outside,), jnp.float32).at[position].set(1.0, mode="drop")
    banded = banded.reshape(nblocks, width_band, BLK, BLK)
    weights = banded.astype(jnp.bfloat16)
    padded = jnp.concatenate([samples[:, P_SIZE - KB * BLK:], samples, samples[:, :KB * BLK]], axis=1)

    def column_product(column):
        window = lax.dynamic_slice_in_dim(padded, column * BLK, width_band * BLK, 1)
        return jnp.dot(window, weights[column].reshape(width_band * BLK, BLK), preferred_element_type=jnp.float32)

    columns = jnp.arange(nblocks, dtype=jnp.int32)
    products = lax.map(column_product, columns)
    products_half = products.astype(jnp.bfloat16)
    flat_half = jnp.transpose(products_half, (1, 0, 2)).reshape(SAMPLES, P_SIZE)
    padded_half = jnp.concatenate([flat_half[:, P_SIZE - KB * BLK:], flat_half, flat_half[:, :KB * BLK]], axis=1)

    def column_gradient(column):
        window_x = lax.dynamic_slice_in_dim(padded, column * BLK, width_band * BLK, 1)
        window_y = lax.dynamic_slice_in_dim(padded_half, column * BLK, width_band * BLK, 1)
        own_x = lax.dynamic_slice_in_dim(samples, column * BLK, BLK, 1)
        first = jnp.dot(window_x.T, products_half[column], preferred_element_type=jnp.float32)
        second = jnp.dot(window_y.T, own_x, preferred_element_type=jnp.float32)
        return (first + second).reshape(width_band, BLK, BLK)

    summed = lax.map(column_gradient, columns)
    identity = jnp.eye(BLK, dtype=jnp.float32)
    diagonals = jnp.diagonal(banded[:, KB], axis1=-2, axis2=-1)
    gradient = summed * (0.5 / SAMPLES)
    gradient = gradient.at[:, KB].add(-identity[None] * (1.0 / diagonals)[:, None, :])
    moved = banded - step_size * gradient
    off_diagonal = jnp.ones((width_band, BLK, BLK), jnp.float32).at[KB].set(1.0 - identity)
    shrunk = jnp.sign(moved) * jnp.maximum(jnp.abs(moved) - step_size * penalty, 0.0)
    updated = jnp.where(off_diagonal > 0.5, shrunk, moved) * present.reshape(nblocks, width_band, 1, 1)
    gathered = updated.reshape(outside, BLK, BLK)[jnp.clip(position, 0, outside - 1)]
    new_omega = gathered * slot_live.astype(jnp.float32)[:, None, None]
    log_sum = jnp.sum(jnp.log(diagonals))
    square_sum = jnp.sum(products * products)
    abs_sum = jnp.sum(jnp.abs(banded * off_diagonal))
    objective = (-log_sum + square_sum / (2.0 * SAMPLES) + penalty * abs_sum) / P_SIZE
    return new_omega, jnp.reshape(objective, (1,)).astype(jnp.float32)
```

```python
import functools

import jax
import jax.numpy as jnp
from jax import lax
from jax.experimental import pallas as pl
from jax.experimental.pallas import tpu as pltpu
from jax.sharding import PartitionSpec as P

P_SIZE = 57344
BLK = 128
KB = 2
SAMPLES = 1024
WB = 2 * KB + 1
WIN = 6 * BLK
PAIR = 2 * BLK

step_size = 0.5
penalty = 0.1

VMEM = pltpu.VMEM
SMEM = pltpu.SMEM
F32 = jnp.float32
BF16 = jnp.bfloat16


def eye_mask():
    r = lax.broadcasted_iota(jnp.int32, (BLK, BLK), 0)
    c = lax.broadcasted_iota(jnp.int32, (BLK, BLK), 1)
    return r == c


def shrunk(om, g, diagonal):
    moved = om - (step_size * 0.5 / SAMPLES) * g
    bound = step_size * penalty
    if not diagonal:
        return moved - jnp.clip(moved, -bound, bound)
    eye = eye_mask()
    on = moved + step_size / jnp.where(eye, om, 1.0)
    return jnp.where(eye, on, moved - jnp.clip(moved, -bound, bound))


def block_at(ref, row, col):
    return ref[row * BLK : (row + 1) * BLK, col * BLK : (col + 1) * BLK]


def band_products(a, window):
    y = lax.dot_general(a, window, (((1,), (1,)), ((), ())), preferred_element_type=F32)
    b = jnp.dot(y.astype(BF16), window, preferred_element_type=F32)
    return y, b


def fold(v):
    rows, lanes = v.shape
    return jnp.sum(v.reshape(rows // 8, 8, lanes), axis=0)


def interior_kernel(
    cb, slots,
    rows_ref, cols_ref, count_ref, x_hbm, om_hbm,
    out_hbm, inv_ref, edge_ref, al_ref, ar_ref, log_ref, sq_ref, abs_ref,
    x, band, bmat, res, zero, a_buf, x_sem, om_sem, out_sem, zero_sem,
):
    npairs = (cb - 2 * KB + 1) // 2
    nblocks = P_SIZE // BLK
    last = cb - 4

    def x_copy(c):
        at = pl.multiple_of(c * BLK, BLK)
        return pltpu.make_async_copy(
            x_hbm.at[:, pl.ds(at, BLK)], x.at[:, pl.ds(at, BLK)], x_sem.at[c]
        )

    for c in range(min(6, cb)):
        x_copy(c).start()

    def clear(p, _):
        inv_ref[p] = -1
        return 0

    lax.fori_loop(0, cb * WB, clear, 0, unroll=5)
    zero[...] = jnp.zeros_like(zero)

    def load_slot(s, _):
        @pl.when(s < count_ref[0])
        def _():
            col = cols_ref[s]
            diff = rows_ref[s] - col + KB
            diff = jnp.where(diff < 0, diff + nblocks, diff)
            diff = jnp.where(diff >= nblocks, diff - nblocks, diff)
            p = lax.rem(col, cb) * WB + diff
            inv_ref[p] = s
            pltpu.make_async_copy(om_hbm.at[s], band.at[p], om_sem.at[p]).start()

        @pl.when(s >= count_ref[0])
        def _():
            pltpu.make_async_copy(zero, out_hbm.at[s], zero_sem.at[s]).start()

        return 0

    lax.fori_loop(0, slots, load_slot, 0)

    for c in range(6, cb):
        x_copy(c).start()

    log_ref[...] = jnp.zeros_like(log_ref)
    sq_ref[...] = jnp.zeros_like(sq_ref)
    abs_ref[...] = jnp.zeros_like(abs_ref)
    a_buf[...] = jnp.zeros_like(a_buf)

    def prepare(c):
        for d in range(WB):
            p = c * WB + d
            slot = inv_ref[p]

            @pl.when(slot >= 0)
            def _():
                pltpu.make_async_copy(om_hbm.at[0], band.at[p], om_sem.at[p]).wait()

            @pl.when(slot < 0)
            def _():
                band[p] = jnp.zeros((BLK, BLK), F32)

        x_copy(c).wait()

    def tally(c):
        eye = eye_mask()
        total = jnp.zeros((8, BLK), F32)
        for d in range(WB):
            v = jnp.abs(band[c * WB + d])
            total += fold(jnp.where(eye, 0.0, v) if d == KB else v)
        abs_ref[...] += total
        diag = jnp.sum(jnp.where(eye, band[c * WB + KB], 0.0), axis=0, keepdims=True)
        log_ref[0:1, :] += jnp.log(diag)

    for c in range(4):
        prepare(c)
        tally(c)

    def outputs(i, delta):
        j = i - delta
        return j * WB + delta + KB, i * WB + KB - delta

    def finish(r0):
        for a in range(2):
            i = r0 + a
            for delta in range(KB + 1):
                j = i - delta
                low, high = outputs(i, delta)
                g = bmat[i * WB + KB - delta] + bmat[j * WB + KB + delta].T
                res[low] = shrunk(band[low], g, delta == 0)
                if delta:
                    res[high] = shrunk(band[high], g.T, False)

    def out_copies(r0, fresh, act):
        for a in range(2):
            i = r0 + a
            for delta in range(KB + 1):
                ok = i - delta >= KB
                if a == 0 and cb % 2:
                    ok = jnp.logical_and(ok, fresh)
                for p in outputs(i, delta)[: 2 if delta else 1]:
                    slot = inv_ref[p]

                    @pl.when(jnp.logical_and(ok, slot >= 0))
                    def _():
                        act(pltpu.make_async_copy(res.at[p], out_hbm.at[slot], out_sem.at[p]))

    def start_of(k):
        return jnp.minimum(KB + 2 * k, last)

    def step(k, _):
        r0 = start_of(k)
        fresh = r0 == KB + 2 * k
        for extra in range(2):
            c = KB + 2 * k + 2 + extra
            if cb % 2:
                pl.when(c < cb)(lambda: prepare(c))
            else:
                prepare(c)
        before = jnp.maximum(start_of(k - 1), KB)
        finish(before)
        for extra in range(2):
            c = KB + 2 * k + 2 + extra
            if cb % 2:
                pl.when(c < cb)(lambda: tally(c))
            else:
                tally(c)
        for a in range(2):
            for w in range(a, a + WB):
                p = (r0 - 2 + w) * WB + a + 4 - w
                a_buf[a * BLK : (a + 1) * BLK, w * BLK : (w + 1) * BLK] = band[p].astype(BF16)
        window = x[:, pl.ds(pl.multiple_of((r0 - 2) * BLK, BLK), WIN)]
        y, b = band_products(a_buf[...], window)
        square = y * y
        second = fold(square[BLK:])
        first = fold(square[:BLK])
        if cb % 2:
            first = jnp.where(fresh, first, 0.0)
        sq_ref[...] += first + second
        for a in range(2):
            for d in range(WB):
                bmat[(r0 + a) * WB + d] = b[
                    a * BLK : (a + 1) * BLK, (a + d) * BLK : (a + d + 1) * BLK
                ]

        @pl.when(k > 0)
        def _():
            out_copies(before, before == KB + 2 * (k - 1), lambda copy: copy.start())

        return 0

    lax.fori_loop(0, npairs, step, 0)
    finish(start_of(npairs - 1))
    out_copies(
        start_of(npairs - 1),
        start_of(npairs - 1) == KB + 2 * (npairs - 1),
        lambda copy: copy.start(),
    )

    e = cb - 2
    for w, (i, j) in enumerate(((2, 0), (2, 1), (3, 1), (e - 2, e), (e - 1, e), (e - 1, e + 1))):
        edge_ref[w] = bmat[i * WB + j - i + KB]

    for ref, base in ((al_ref, 0), (ar_ref, e)):
        ref[...] = jnp.zeros_like(ref)
        for a in range(2):
            for w in range(a, a + WB):
                j, i = base + a, base - 2 + w
                if 0 <= i < cb:
                    v = band[i * WB + j - i + KB]
                else:
                    v = band[j * WB + i - j + KB].T
                ref[a * BLK : (a + 1) * BLK, w * BLK : (w + 1) * BLK] = v.astype(BF16)

    def drain(k, _):
        r0 = start_of(k)
        out_copies(r0, r0 == KB + 2 * k, lambda copy: copy.wait())
        return 0

    lax.fori_loop(0, npairs, drain, 0)

    def drain_zero(s, _):
        pltpu.make_async_copy(zero, out_hbm.at[s], zero_sem.at[s]).wait()
        return 0

    lax.fori_loop(count_ref[0], slots, drain_zero, 0)


def edge_kernel(
    n, cb,
    x_hbm, hl_hbm, hr_hbm, al, ar, log_in, sq_in, abs_in,
    bl, br, from_left, from_right, sums_out,
    xl, xr, out_l, out_r, in_l, in_r, tile, tiles, load_sem, send_sem, recv_sem, tsend, trecv,
):
    me = lax.axis_index("var")
    right, left = lax.rem(me + 1, n), lax.rem(me + n - 1, n)
    barrier = pltpu.get_barrier_semaphore()

    def greet(k, _):
        pl.semaphore_signal(
            barrier, inc=1, device_id={"var": lax.rem(me + k, n)},
            device_id_type=pl.DeviceIdType.MESH,
        )
        return 0

    lax.fori_loop(1, n, greet, 0)
    width = cb * BLK
    loads = [
        pltpu.make_async_copy(src, dst, load_sem.at[k])
        for k, (src, dst) in enumerate(
            (
                (hl_hbm, xl.at[:, 0:PAIR]),
                (x_hbm.at[:, 0 : 2 * PAIR], xl.at[:, PAIR:WIN]),
                (x_hbm.at[:, width - 2 * PAIR : width], xr.at[:, 0 : 2 * PAIR]),
                (hr_hbm, xr.at[:, 2 * PAIR : WIN]),
            )
        )
    ]
    for load in loads:
        load.start()
    loads[0].wait()
    loads[1].wait()
    y, b = band_products(al[...], xl[...])
    square = fold(y * y)
    bl[...] = b
    for w, (row, col) in enumerate(((0, 0), (0, 1), (1, 1))):
        out_l[w] = block_at(b, row, col).astype(BF16)
    loads[2].wait()
    loads[3].wait()
    y, b = band_products(ar[...], xr[...])
    square = square + fold(y * y) + sq_in[...]
    br[...] = b
    for w, (row, col) in enumerate(((0, 4), (1, 4), (1, 5))):
        out_r[w] = block_at(b, row, col).astype(BF16)

    lanes = square[:, 0:BLK]
    for k in range(1, SAMPLES // BLK):
        lanes = lanes + square[:, k * BLK : (k + 1) * BLK]
    tile[...] = jnp.zeros_like(tile)
    tile[0:1, :] = jnp.sum(log_in[...], axis=0, keepdims=True)
    tile[1:2, :] = jnp.sum(lanes, axis=0, keepdims=True)
    tile[2:3, :] = jnp.sum(abs_in[...], axis=0, keepdims=True)

    pl.semaphore_wait(barrier, n - 1)
    to_left = pltpu.make_async_remote_copy(
        src_ref=out_l, dst_ref=in_r, send_sem=send_sem.at[0], recv_sem=recv_sem.at[0],
        device_id={"var": left}, device_id_type=pl.DeviceIdType.MESH,
    )
    to_right = pltpu.make_async_remote_copy(
        src_ref=out_r, dst_ref=in_l, send_sem=send_sem.at[1], recv_sem=recv_sem.at[1],
        device_id={"var": right}, device_id_type=pl.DeviceIdType.MESH,
    )
    to_left.start()
    to_right.start()

    def tile_copy(k):
        return pltpu.make_async_remote_copy(
            src_ref=tile, dst_ref=tiles.at[k], send_sem=tsend.at[k], recv_sem=trecv.at[k],
            device_id={"var": lax.rem(me + k, n)}, device_id_type=pl.DeviceIdType.MESH,
        )

    def send_tile(k, _):
        tile_copy(k).start()
        return 0

    lax.fori_loop(1, n, send_tile, 0)

    def wait_tile(k, _):
        tile_copy(k).wait()
        return 0

    lax.fori_loop(1, n, wait_tile, 0)
    total = tile[...]
    for k in range(1, n):
        total = total + tiles[k]
    sums_out[...] = total
    to_left.wait()
    to_right.wait()
    from_left[...] = in_l[...]
    from_right[...] = in_r[...]


def finish_kernel(
    cb,
    inv_ref, sums, bl, br, edge, from_left, from_right, om_hbm, out_in,
    out_hbm, obj_ref,
    om, res, om_sem, out_sem,
):
    del out_in
    e = cb - 2
    pairs = [(0, 0), (0, 1), (1, 1), (0, 2), (1, 2), (1, 3), (-2, 0), (-1, 0), (-1, 1)]
    pairs += [(e, e), (e, e + 1), (e + 1, e + 1), (e - 2, e), (e - 1, e), (e - 1, e + 1)]
    pairs += [(e, e + 2), (e + 1, e + 2), (e + 1, e + 3)]
    left_in = {(-2, 0): 0, (-1, 0): 1, (-1, 1): 2}
    right_in = {(e + 2, e): 0, (e + 2, e + 1): 1, (e + 3, e + 1): 2}
    inner = {(2, 0): 0, (2, 1): 1, (3, 1): 2, (e - 2, e): 3, (e - 1, e): 4, (e - 1, e + 1): 5}

    def term(i, j):
        if (i, j) in left_in:
            return from_left[left_in[i, j]].astype(F32)
        if (i, j) in right_in:
            return from_right[right_in[i, j]].astype(F32)
        if (i, j) in inner:
            return edge[inner[i, j]]
        if i in (0, 1):
            return block_at(bl, i, j + 2)
        return block_at(br, i - e, j - e + 2)

    writes = []
    for i, j in pairs:
        if 0 <= j < cb:
            writes.append((i, j))
        if i != j and 0 <= i < cb:
            writes.append((j, i))
    index = {key: w for w, key in enumerate(writes)}
    slot_of = [inv_ref[j * WB + i - j + KB] for i, j in writes]

    def load(w):
        return pltpu.make_async_copy(om_hbm.at[jnp.maximum(slot_of[w], 0)], om.at[w], om_sem.at[w])

    def store(w):
        return pltpu.make_async_copy(res.at[w], out_hbm.at[slot_of[w]], out_sem.at[w])

    for w in range(len(writes)):
        load(w).start()
    lane = jnp.sum(sums[...], axis=1, keepdims=True)
    log_sum, square_sum, abs_sum = lane[0:1, :], lane[1:2, :], lane[2:3, :]
    value = (-log_sum + square_sum / (2.0 * SAMPLES) + penalty * abs_sum) / P_SIZE
    obj_ref[0] = jnp.sum(value)
    for w in range(len(writes)):
        load(w).wait()
    for i, j in pairs:
        g = term(i, j) + term(j, i).T
        if (i, j) in index:
            w = index[i, j]
            res[w] = shrunk(om[w], g, i == j)
        if i != j and (j, i) in index:
            w = index[j, i]
            res[w] = shrunk(om[w], g.T, False)
    for w in range(len(writes)):
        pl.when(slot_of[w] >= 0)(lambda: store(w).start())
    for w in range(len(writes)):
        pl.when(slot_of[w] >= 0)(lambda: store(w).wait())


def on_device(samples, omega, block_rows, block_cols, block_count):
    n = lax.axis_size("var")
    count, width = samples.shape
    cb = width // BLK
    slots = omega.shape[0]
    whole = pl.BlockSpec(memory_space=VMEM)
    scalar = pl.BlockSpec(memory_space=SMEM)
    anywhere = pl.BlockSpec(memory_space=pl.ANY)

    def shape(dims, kind=F32):
        return jax.ShapeDtypeStruct(dims, kind)

    halo_left = lax.ppermute(
        samples[:, width - PAIR :], "var", [(i, (i + 1) % n) for i in range(n)]
    )
    halo_right = lax.ppermute(
        samples[:, :PAIR], "var", [((i + 1) % n, i) for i in range(n)]
    )

    out, inv, edge, al, ar, logs, squares, sizes = pl.pallas_call(
        functools.partial(interior_kernel, cb, slots),
        out_shape=(
            shape((slots, BLK, BLK)), shape((cb * WB,), jnp.int32), shape((6, BLK, BLK)),
            shape((PAIR, WIN), BF16), shape((PAIR, WIN), BF16),
            shape((8, BLK)), shape((8, count)), shape((8, BLK)),
        ),
        in_specs=[scalar, scalar, scalar, anywhere, anywhere],
        out_specs=(anywhere, scalar, whole, whole, whole, whole, whole, whole),
        scratch_shapes=[
            VMEM((count, width), BF16),
            VMEM((cb * WB, BLK, BLK), F32),
            VMEM((cb * WB, BLK, BLK), F32),
            VMEM((cb * WB, BLK, BLK), F32),
            VMEM((BLK, BLK), F32),
            VMEM((PAIR, WIN), BF16),
            pltpu.SemaphoreType.DMA((cb,)),
            pltpu.SemaphoreType.DMA((cb * WB,)),
            pltpu.SemaphoreType.DMA((cb * WB,)),
            pltpu.SemaphoreType.DMA((slots,)),
        ],
        cost_estimate=pl.CostEstimate(
            flops=4 * cb * count * BLK * WIN,
            bytes_accessed=2 * count * width + 8 * slots * BLK * BLK,
            transcendentals=width,
        ),
        compiler_params=pltpu.CompilerParams(vmem_limit_bytes=50 * 2**20),
        name="interior",
    )(block_rows, block_cols, block_count, samples, omega)

    bl, br, from_left, from_right, sums = pl.pallas_call(
        functools.partial(edge_kernel, n, cb),
        out_shape=(
            shape((PAIR, WIN)), shape((PAIR, WIN)),
            shape((3, BLK, BLK), BF16), shape((3, BLK, BLK), BF16), shape((8, BLK)),
        ),
        in_specs=[anywhere] * 3 + [whole] * 5,
        out_specs=(whole,) * 5,
        scratch_shapes=[
            VMEM((count, WIN), BF16),
            VMEM((count, WIN), BF16),
            VMEM((3, BLK, BLK), BF16),
            VMEM((3, BLK, BLK), BF16),
            VMEM((3, BLK, BLK), BF16),
            VMEM((3, BLK, BLK), BF16),
            VMEM((8, BLK), F32),
            VMEM((n, 8, BLK), F32),
            pltpu.SemaphoreType.DMA((4,)),
            pltpu.SemaphoreType.DMA((2,)),
            pltpu.SemaphoreType.DMA((2,)),
            pltpu.SemaphoreType.DMA((n,)),
            pltpu.SemaphoreType.DMA((n,)),
        ],
        cost_estimate=pl.CostEstimate(
            flops=8 * count * PAIR * WIN, bytes_accessed=8 * count * WIN, transcendentals=0
        ),
        compiler_params=pltpu.CompilerParams(
            collective_id=0, has_side_effects=True, vmem_limit_bytes=40 * 2**20
        ),
        name="edges",
    )(samples, halo_left, halo_right, al, ar, logs, squares, sizes)

    new_omega, objective = pl.pallas_call(
        functools.partial(finish_kernel, cb),
        out_shape=(shape((slots, BLK, BLK)), shape((1,))),
        in_specs=[scalar] + [whole] * 6 + [anywhere] * 2,
        out_specs=(anywhere, scalar),
        scratch_shapes=[
            VMEM((26, BLK, BLK), F32),
            VMEM((26, BLK, BLK), F32),
            pltpu.SemaphoreType.DMA((26,)),
            pltpu.SemaphoreType.DMA((26,)),
        ],
        input_output_aliases={8: 0},
        compiler_params=pltpu.CompilerParams(vmem_limit_bytes=40 * 2**20),
        name="outer_blocks",
    )(inv, sums, bl, br, edge, from_left, from_right, omega, out)
    return new_omega, objective


def solution(mesh):
    placed = (
        P("groups", "var"),
        P(("groups", "var"), None, None),
        P(("groups", "var")),
        P(("groups", "var")),
        P(("groups", "var")),
    )
    return jax.shard_map(
        on_device,
        mesh=mesh,
        in_specs=placed,
        out_specs=(P(("groups", "var"), None, None), P("groups")),
        check_vma=False,
    )
```

```python
import functools

import jax
import jax.numpy as jnp
from jax import lax
from jax.experimental import pallas as pl
from jax.experimental.pallas import tpu as pltpu
from jax.sharding import PartitionSpec as P

P_SIZE = 57344
BLK = 128
KB = 2
SAMPLES = 1024
WB = 2 * KB + 1
WIN = 6 * BLK
PAIR = 2 * BLK

step_size = 0.5
penalty = 0.1

VMEM = pltpu.VMEM
SMEM = pltpu.SMEM
F32 = jnp.float32
BF16 = jnp.bfloat16


def eye_mask():
    r = lax.broadcasted_iota(jnp.int32, (BLK, BLK), 0)
    c = lax.broadcasted_iota(jnp.int32, (BLK, BLK), 1)
    return r == c


def shrunk(om, g, diagonal):
    moved = om - (step_size * 0.5 / SAMPLES) * g
    bound = step_size * penalty
    if not diagonal:
        return moved - jnp.clip(moved, -bound, bound)
    eye = eye_mask()
    on = moved + step_size / jnp.where(eye, om, 1.0)
    return jnp.where(eye, on, moved - jnp.clip(moved, -bound, bound))


def block_at(ref, row, col):
    return ref[row * BLK : (row + 1) * BLK, col * BLK : (col + 1) * BLK]


def band_products(a, window):
    y = lax.dot_general(a, window, (((1,), (1,)), ((), ())), preferred_element_type=F32)
    b = jnp.dot(y.astype(BF16), window, preferred_element_type=F32)
    return y, b


def outer_pairs(cb):
    e = cb - 2
    pairs = [(0, 0), (0, 1), (1, 1), (0, 2), (1, 2), (1, 3), (-2, 0), (-1, 0), (-1, 1)]
    pairs += [(e, e), (e, e + 1), (e + 1, e + 1), (e - 2, e), (e - 1, e), (e - 1, e + 1)]
    pairs += [(e, e + 2), (e + 1, e + 2), (e + 1, e + 3)]
    writes = []
    for i, j in pairs:
        if 0 <= j < cb:
            writes.append((i, j))
        if i != j and 0 <= i < cb:
            writes.append((j, i))
    return pairs, writes


def fold(v):
    rows, lanes = v.shape
    return jnp.sum(v.reshape(rows // 8, 8, lanes), axis=0)


def interior_kernel(
    cb, slots, chunk,
    rows_hbm, cols_hbm, count_ref, x_hbm, om_hbm,
    out_hbm, inv_ref, edge_ref, om_edge_ref, al_ref, ar_ref, log_ref, sq_ref, abs_ref,
    rows_ref, cols_ref, ready, x, om, bmat, res, a_buf, tab_sem, x_sem, om_sem, out_sem,
):
    npairs = (cb - 2 * KB + 1) // 2
    nblocks = P_SIZE // BLK
    chunks = slots // chunk
    last = cb - 4

    def x_copy(c):
        at = pl.multiple_of(c * BLK, BLK)
        return pltpu.make_async_copy(
            x_hbm.at[:, pl.ds(at, BLK)], x.at[:, pl.ds(at, BLK)], x_sem.at[c]
        )

    def om_copy(m):
        part = pl.ds(m * chunk, chunk)
        return pltpu.make_async_copy(om_hbm.at[part], om.at[part], om_sem.at[m])

    def out_copy(m):
        part = pl.ds(m * chunk, chunk)
        return pltpu.make_async_copy(res.at[part], out_hbm.at[part], out_sem.at[m])

    tables = [
        pltpu.make_async_copy(rows_hbm, rows_ref, tab_sem.at[0]),
        pltpu.make_async_copy(cols_hbm, cols_ref, tab_sem.at[1]),
    ]
    for table in tables:
        table.start()
    xs = oms = 0
    while xs < cb or oms < chunks:
        if oms < chunks:
            om_copy(oms).start()
            oms += 1
        for _ in range(-(-cb // chunks) + (xs == 0)):
            if xs < cb:
                x_copy(xs).start()
                xs += 1

    def clear(p, _):
        inv_ref[p] = slots
        return 0

    lax.fori_loop(0, cb * WB + 1, clear, 0, unroll=4)
    for m in range(chunks):
        ready[m] = 0
    om[slots] = jnp.zeros((BLK, BLK), F32)
    log_ref[...] = jnp.zeros_like(log_ref)
    sq_ref[...] = jnp.zeros_like(sq_ref)
    abs_ref[...] = jnp.zeros_like(abs_ref)
    a_buf[...] = jnp.zeros_like(a_buf)
    count = count_ref[0]

    def no_block(s, _):
        res[s] = jnp.zeros((BLK, BLK), F32)
        return 0

    lax.fori_loop(count, slots, no_block, 0)
    for table in tables:
        table.wait()

    def place(m, t):
        s = m * chunk + t
        col = cols_ref[s]
        diff = rows_ref[s] - col
        diff = jnp.where(diff < -KB, diff + nblocks, diff)
        diff = jnp.where(diff > KB, diff - nblocks, diff)
        j = lax.rem(col, cb)
        live = s < count
        inv_ref[jnp.where(live, j * WB + diff + KB, cb * WB)] = s
        later = jnp.maximum(j, j + diff)
        return jnp.where(live, later, 0)

    def place_chunk(m, _):
        later = place(m, 0)
        for t in range(1, chunk):
            later = jnp.maximum(later, place(m, t))
        done = (later - KB) // 2
        if cb % 2:
            done = jnp.where(later >= last, npairs - 1, done)
        ready[m] = jnp.clip(done, 0, npairs - 1)
        return 0

    lax.fori_loop(0, chunks, place_chunk, 0)

    def slot_at(i, j):
        return inv_ref[j * WB + i - j + KB]

    def arrive(c, have):
        x_copy(c).wait()
        most = jnp.int32(-1)
        for d in range(WB):
            slot = inv_ref[c * WB + d]
            most = jnp.maximum(most, jnp.where(slot < slots, slot, -1))
        upto = (most + chunk) // chunk

        def wait(m, _):
            om_copy(m).wait()
            return 0

        lax.fori_loop(have, upto, wait, 0)
        return jnp.maximum(have, upto)

    def tally(c):
        eye = eye_mask()
        total = jnp.zeros((8, BLK), F32)
        for d in range(WB):
            v = om[inv_ref[c * WB + d]]
            if d == KB:
                diag = jnp.sum(jnp.where(eye, v, 0.0), axis=0, keepdims=True)
                v = jnp.where(eye, 0.0, v)
            total += fold(jnp.abs(v))
        abs_ref[...] += total
        log_ref[0:1, :] += jnp.log(diag)

    have = jnp.int32(0)
    for c in range(4):
        have = arrive(c, have)
    for c in range(4):
        tally(c)

    def finish(r0):
        for a in range(2):
            i = r0 + a
            for delta in range(KB + 1):
                j = i - delta
                low, high = slot_at(i, j), slot_at(j, i)
                g = bmat[i * WB + KB - delta] + bmat[j * WB + KB + delta].T
                res[low] = shrunk(om[low], g, delta == 0)
                if delta:
                    res[high] = shrunk(om[high], g.T, False)

    def start_of(k):
        return jnp.minimum(KB + 2 * k, last)

    def send(k, sent):
        def more(m):
            return jnp.logical_and(m < chunks, ready[jnp.minimum(m, chunks - 1)] <= k)

        def start(m):
            out_copy(m).start()
            return m + 1

        return lax.while_loop(more, start, sent)

    def step(k, carry):
        have, sent = carry
        r0 = start_of(k)
        fresh = r0 == KB + 2 * k
        for extra in range(2):
            c = KB + 2 * k + 2 + extra
            if cb % 2:
                have = lax.cond(c < cb, functools.partial(arrive, c), lambda h: h, have)
            else:
                have = arrive(c, have)
        before = jnp.maximum(start_of(k - 1), KB)
        for a in range(2):
            for w in range(a, a + WB):
                a_buf[a * BLK : (a + 1) * BLK, w * BLK : (w + 1) * BLK] = om[
                    slot_at(r0 + a, r0 - 2 + w)
                ].astype(BF16)
        finish(before)
        for extra in range(2):
            c = KB + 2 * k + 2 + extra
            if cb % 2:
                pl.when(c < cb)(functools.partial(tally, c))
            else:
                tally(c)
        window = x[:, pl.ds(pl.multiple_of((r0 - 2) * BLK, BLK), WIN)]
        y, b = band_products(a_buf[...], window)
        square = y * y
        second = fold(square[BLK:])
        first = fold(square[:BLK])
        if cb % 2:
            first = jnp.where(fresh, first, 0.0)
        sq_ref[...] += first + second
        for a in range(2):
            for d in range(WB):
                bmat[(r0 + a) * WB + d] = b[
                    a * BLK : (a + 1) * BLK, (a + d) * BLK : (a + d + 1) * BLK
                ]
        return have, send(k - 1, sent)

    have, sent = lax.fori_loop(0, npairs, step, (have, jnp.int32(0)))
    finish(start_of(npairs - 1))
    send(npairs - 1, sent)

    def late(m, _):
        om_copy(m).wait()
        return 0

    lax.fori_loop(have, chunks, late, 0)
    e = cb - 2
    for w, (i, j) in enumerate(((2, 0), (2, 1), (3, 1), (e - 2, e), (e - 1, e), (e - 1, e + 1))):
        edge_ref[w] = bmat[i * WB + j - i + KB]

    for w, (i, j) in enumerate(outer_pairs(cb)[1]):
        om_edge_ref[w] = om[slot_at(i, j)]

    for ref, base in ((al_ref, 0), (ar_ref, e)):
        ref[...] = jnp.zeros_like(ref)
        for a in range(2):
            for w in range(a, a + WB):
                j, i = base + a, base - 2 + w
                v = om[slot_at(j, i)] if 0 <= i < cb else om[slot_at(i, j)].T
                ref[a * BLK : (a + 1) * BLK, w * BLK : (w + 1) * BLK] = v.astype(BF16)

    for m in range(chunks):
        out_copy(m).wait()


def edge_kernel(
    n, cb,
    x_hbm, hl_hbm, hr_hbm, al, ar, log_in, sq_in, abs_in,
    bl, br, from_left, from_right, sums_out,
    xl, xr, out_l, out_r, in_l, in_r, tile, tiles, load_sem, send_sem, recv_sem, tsend, trecv,
):
    me = lax.axis_index("var")
    right, left = lax.rem(me + 1, n), lax.rem(me + n - 1, n)
    barrier = pltpu.get_barrier_semaphore()

    def greet(k, _):
        pl.semaphore_signal(
            barrier, inc=1, device_id={"var": lax.rem(me + k, n)},
            device_id_type=pl.DeviceIdType.MESH,
        )
        return 0

    lax.fori_loop(1, n, greet, 0)
    width = cb * BLK
    loads = [
        pltpu.make_async_copy(src, dst, load_sem.at[k])
        for k, (src, dst) in enumerate(
            (
                (hl_hbm, xl.at[:, 0:PAIR]),
                (x_hbm.at[:, 0 : 2 * PAIR], xl.at[:, PAIR:WIN]),
                (x_hbm.at[:, width - 2 * PAIR : width], xr.at[:, 0 : 2 * PAIR]),
                (hr_hbm, xr.at[:, 2 * PAIR : WIN]),
            )
        )
    ]
    for load in loads:
        load.start()
    loads[0].wait()
    loads[1].wait()
    y, b = band_products(al[...], xl[...])
    square = fold(y * y)
    bl[...] = b
    for w, (row, col) in enumerate(((0, 0), (0, 1), (1, 1))):
        out_l[w] = block_at(b, row, col).astype(BF16)
    loads[2].wait()
    loads[3].wait()
    y, b = band_products(ar[...], xr[...])
    square = square + fold(y * y) + sq_in[...]
    br[...] = b
    for w, (row, col) in enumerate(((0, 4), (1, 4), (1, 5))):
        out_r[w] = block_at(b, row, col).astype(BF16)

    lanes = square[:, 0:BLK]
    for k in range(1, SAMPLES // BLK):
        lanes = lanes + square[:, k * BLK : (k + 1) * BLK]
    tile[...] = jnp.zeros_like(tile)
    tile[0:1, :] = jnp.sum(log_in[...], axis=0, keepdims=True)
    tile[1:2, :] = jnp.sum(lanes, axis=0, keepdims=True)
    tile[2:3, :] = jnp.sum(abs_in[...], axis=0, keepdims=True)

    pl.semaphore_wait(barrier, n - 1)
    to_left = pltpu.make_async_remote_copy(
        src_ref=out_l, dst_ref=in_r, send_sem=send_sem.at[0], recv_sem=recv_sem.at[0],
        device_id={"var": left}, device_id_type=pl.DeviceIdType.MESH,
    )
    to_right = pltpu.make_async_remote_copy(
        src_ref=out_r, dst_ref=in_l, send_sem=send_sem.at[1], recv_sem=recv_sem.at[1],
        device_id={"var": right}, device_id_type=pl.DeviceIdType.MESH,
    )
    to_left.start()
    to_right.start()

    def tile_copy(k):
        return pltpu.make_async_remote_copy(
            src_ref=tile, dst_ref=tiles.at[k], send_sem=tsend.at[k], recv_sem=trecv.at[k],
            device_id={"var": lax.rem(me + k, n)}, device_id_type=pl.DeviceIdType.MESH,
        )

    def send_tile(k, _):
        tile_copy(k).start()
        return 0

    lax.fori_loop(1, n, send_tile, 0)

    def wait_tile(k, _):
        tile_copy(k).wait()
        return 0

    lax.fori_loop(1, n, wait_tile, 0)
    total = tile[...]
    for k in range(1, n):
        total = total + tiles[k]
    sums_out[...] = total
    to_left.wait()
    to_right.wait()
    from_left[...] = in_l[...]
    from_right[...] = in_r[...]


def finish_kernel(
    cb, slots,
    inv_ref, sums, bl, br, edge, from_left, from_right, om, out_in,
    out_hbm, obj_ref,
    res, out_sem,
):
    del out_in
    e = cb - 2
    pairs, writes = outer_pairs(cb)
    left_in = {(-2, 0): 0, (-1, 0): 1, (-1, 1): 2}
    right_in = {(e + 2, e): 0, (e + 2, e + 1): 1, (e + 3, e + 1): 2}
    inner = {(2, 0): 0, (2, 1): 1, (3, 1): 2, (e - 2, e): 3, (e - 1, e): 4, (e - 1, e + 1): 5}

    def term(i, j):
        if (i, j) in left_in:
            return from_left[left_in[i, j]].astype(F32)
        if (i, j) in right_in:
            return from_right[right_in[i, j]].astype(F32)
        if (i, j) in inner:
            return edge[inner[i, j]]
        if i in (0, 1):
            return block_at(bl, i, j + 2)
        return block_at(br, i - e, j - e + 2)

    index = {key: w for w, key in enumerate(writes)}
    slot_of = [inv_ref[j * WB + i - j + KB] for i, j in writes]

    def store(w):
        return pltpu.make_async_copy(res.at[w], out_hbm.at[slot_of[w]], out_sem.at[w])

    lane = jnp.sum(sums[...], axis=1, keepdims=True)
    log_sum, square_sum, abs_sum = lane[0:1, :], lane[1:2, :], lane[2:3, :]
    value = (-log_sum + square_sum / (2.0 * SAMPLES) + penalty * abs_sum) / P_SIZE
    obj_ref[0] = jnp.sum(value)
    for i, j in pairs:
        g = term(i, j) + term(j, i).T
        if (i, j) in index:
            w = index[i, j]
            res[w] = shrunk(om[w], g, i == j)
        if i != j and (j, i) in index:
            w = index[j, i]
            res[w] = shrunk(om[w], g.T, False)
    for w in range(len(writes)):
        pl.when(slot_of[w] < slots)(lambda: store(w).start())
    for w in range(len(writes)):
        pl.when(slot_of[w] < slots)(lambda: store(w).wait())


def on_device(samples, omega, block_rows, block_cols, block_count):
    n = lax.axis_size("var")
    count, width = samples.shape
    cb = width // BLK
    slots = omega.shape[0]
    chunk = 2 * WB if slots % (2 * WB) == 0 else WB
    whole = pl.BlockSpec(memory_space=VMEM)
    scalar = pl.BlockSpec(memory_space=SMEM)
    anywhere = pl.BlockSpec(memory_space=pl.ANY)
    hbm = pl.BlockSpec(memory_space=pltpu.HBM)

    def shape(dims, kind=F32):
        return jax.ShapeDtypeStruct(dims, kind)

    halo_left = lax.ppermute(
        samples[:, width - PAIR :], "var", [(i, (i + 1) % n) for i in range(n)]
    )
    halo_right = lax.ppermute(
        samples[:, :PAIR], "var", [((i + 1) % n, i) for i in range(n)]
    )

    out, inv, edge, omega_edge, al, ar, logs, squares, sizes = pl.pallas_call(
        functools.partial(interior_kernel, cb, slots, chunk),
        out_shape=(
            shape((slots, BLK, BLK)), shape((cb * WB + 1,), jnp.int32), shape((6, BLK, BLK)),
            shape((26, BLK, BLK)),
            shape((PAIR, WIN), BF16), shape((PAIR, WIN), BF16),
            shape((8, BLK)), shape((8, count)), shape((8, BLK)),
        ),
        in_specs=[hbm, hbm, scalar, hbm, hbm],
        out_specs=(anywhere, scalar) + (whole,) * 7,
        scratch_shapes=[
            SMEM((slots,), jnp.int32),
            SMEM((slots,), jnp.int32),
            SMEM((slots // chunk,), jnp.int32),
            VMEM((count, width), BF16),
            VMEM((slots + 1, BLK, BLK), F32),
            VMEM((cb * WB, BLK, BLK), F32),
            VMEM((slots + 1, BLK, BLK), F32),
            VMEM((PAIR, WIN), BF16),
            pltpu.SemaphoreType.DMA((2,)),
            pltpu.SemaphoreType.DMA((cb,)),
            pltpu.SemaphoreType.DMA((slots // chunk,)),
            pltpu.SemaphoreType.DMA((slots // chunk,)),
        ],
        cost_estimate=pl.CostEstimate(
            flops=4 * cb * count * BLK * WIN,
            bytes_accessed=2 * count * width + 8 * slots * BLK * BLK,
            transcendentals=width,
        ),
        compiler_params=pltpu.CompilerParams(vmem_limit_bytes=50 * 2**20),
        name="interior",
    )(block_rows, block_cols, block_count, samples, omega)

    bl, br, from_left, from_right, sums = pl.pallas_call(
        functools.partial(edge_kernel, n, cb),
        out_shape=(
            shape((PAIR, WIN)), shape((PAIR, WIN)),
            shape((3, BLK, BLK), BF16), shape((3, BLK, BLK), BF16), shape((8, BLK)),
        ),
        in_specs=[hbm] + [anywhere] * 2 + [whole] * 5,
        out_specs=(whole,) * 5,
        scratch_shapes=[
            VMEM((count, WIN), BF16),
            VMEM((count, WIN), BF16),
            VMEM((3, BLK, BLK), BF16),
            VMEM((3, BLK, BLK), BF16),
            VMEM((3, BLK, BLK), BF16),
            VMEM((3, BLK, BLK), BF16),
            VMEM((8, BLK), F32),
            VMEM((n, 8, BLK), F32),
            pltpu.SemaphoreType.DMA((4,)),
            pltpu.SemaphoreType.DMA((2,)),
            pltpu.SemaphoreType.DMA((2,)),
            pltpu.SemaphoreType.DMA((n,)),
            pltpu.SemaphoreType.DMA((n,)),
        ],
        cost_estimate=pl.CostEstimate(
            flops=8 * count * PAIR * WIN, bytes_accessed=8 * count * WIN, transcendentals=0
        ),
        compiler_params=pltpu.CompilerParams(
            collective_id=0, has_side_effects=True, vmem_limit_bytes=40 * 2**20
        ),
        name="edges",
    )(samples, halo_left, halo_right, al, ar, logs, squares, sizes)

    new_omega, objective = pl.pallas_call(
        functools.partial(finish_kernel, cb, slots),
        out_shape=(shape((slots, BLK, BLK)), shape((1,))),
        in_specs=[scalar] + [whole] * 7 + [anywhere],
        out_specs=(anywhere, scalar),
        scratch_shapes=[
            VMEM((26, BLK, BLK), F32),
            pltpu.SemaphoreType.DMA((26,)),
        ],
        input_output_aliases={8: 0},
        compiler_params=pltpu.CompilerParams(vmem_limit_bytes=40 * 2**20),
        name="outer_blocks",
    )(inv, sums, bl, br, edge, from_left, from_right, omega_edge, out)
    return new_omega, objective


def solution(mesh):
    placed = (
        P("groups", "var"),
        P(("groups", "var"), None, None),
        P(("groups", "var")),
        P(("groups", "var")),
        P(("groups", "var")),
    )
    return jax.shard_map(
        on_device,
        mesh=mesh,
        in_specs=placed,
        out_specs=(P(("groups", "var"), None, None), P("groups")),
        check_vma=False,
    )
```
